32 devices in a mesh: section: 2 (over x), dp: 8 (over z, core), tensor: 2 (over y).
Axes of the slice: x: 2, y: 2, z: 4, core: 2. Of those that a mesh axis runs over, the one named last changes fastest.
Arguments:
- inputs: bfloat16 [4, 3328, 768], P(None, 'dp'), may hold values from -6 to 6
- segments: int32 [4, 3328], P(None, 'dp'), may hold values from 0 to 31, never falling along the last dimension, each value on 1 to 416 neighbouring positions
- cotangent: bfloat16 [4, 3328, 768], P(None, 'dp'), may hold values from -6 to 6
- query_weight: bfloat16 [2, 768, 768], P('section', None, 'tensor'), may hold values from -0.21875 to 0.21875
- key_weight: bfloat16 [2, 768, 768], P('section', None, 'tensor'), may hold values from -0.21875 to 0.21875
- value_weight: bfloat16 [2, 768, 768], P('section', None, 'tensor'), may hold values from -0.21875 to 0.21875
- out_weight: bfloat16 [2, 768, 768], P('section', 'tensor'), may hold values from -0.625 to 0.625
- hidden_weight: bfloat16 [2, 768, 3072], P('section', None, 'tensor'), may hold values from -0.21875 to 0.21875
- down_weight: bfloat16 [2, 3072, 768], P('section', 'tensor'), may hold values from -0.109375 to 0.109375
- first_gain: float32 [2, 768], P('section'), may hold values from 0.5 to 1.5
- second_gain: float32 [2, 768], P('section'), may hold values from 0.5 to 1.5
- query_down: bfloat16 [2, 768, 8], P('section'), may hold values from -0.21875 to 0.21875
- query_up: bfloat16 [2, 8, 768], P('section', None, 'tensor'), may hold values from -2 to 2
- value_down: bfloat16 [2, 768, 8], P('section'), may hold values from -0.21875 to 0.21875
- value_up: bfloat16 [2, 8, 768], P('section', None, 'tensor'), may hold values from -2 to 2
Outputs:
- activations: bfloat16 [2, 4, 3328, 768], P('section', None, ('dp', 'tensor'))
- input_grads: bfloat16 [2, 4, 3328, 768], P('section', None, ('dp', 'tensor'))
- query_down_grad: float32 [2, 768, 8], P('section')
- query_up_grad: float32 [2, 8, 768], P('section', None, 'tensor')
- value_down_grad: float32 [2, 768, 8], P('section')
- value_up_grad: float32 [2, 8, 768], P('section', None, 'tensor')
The draws below stay inside these ranges and needn't reach their ends.
Inputs may be any that keep to these rules, and one draw needn't show every extreme that they name: `segments`: along the tokens of a micro-batch the segment numbers never fall; each segment holds 1 to 416 tokens and one holds exactly 416.
All inputs are finite; a program needn't handle non-finite values.
Results may differ from the reference program's by a relative error of at most 0.035.
Values may be sent and summed in bfloat16 or wider, within the bound.
No kernel may reach another device: no remote copies, remote signals or barrier semaphores. Data moves between devices by JAX's collectives and lax.ppermute only.
A program may use at most 192 MiB of HBM per device.

```python
import math
import jax
import jax.numpy as jnp
import numpy as np
from jax import lax

D = 768
HEAD_DIM = 64
FF = 3072
RANK = 8
PACK = 416
MICRO = 4
TOKENS = 3328


def block_levels(own_key, dims, pieces, low, top_value):
    def one(axis_at, blocks):
        heights = jax.random.uniform(jax.random.fold_in(jax.random.fold_in(own_key, 6), axis_at), (blocks,), jnp.float32, low / len(pieces), top_value / len(pieces))
        return jnp.repeat(jnp.exp(heights), dims[axis_at] // blocks).reshape((-1,) + (1,) * (len(dims) - axis_at - 1))

    level = one(*pieces[0])
    for cut in pieces[1:]:
        level = level * one(*cut)
    return level


def length_profile(number_of, total, limit, slope):
    portions = [(1 << 20) // math.isqrt(grade ** slope) + 1 for grade in range(2, number_of + 1)]
    rest, given = total - limit - (number_of - 1), [1] * (number_of - 1)
    while rest > 0:
        candidates = [i for i in range(number_of - 1) if given[i] < limit]
        pool, budget = sum([portions[i] for i in candidates]), rest
        for i in candidates:
            extra = min(limit - given[i], max(1, budget * portions[i] // pool), rest)
            given[i] = given[i] + extra
            rest = rest - extra
    return np.array([limit] + given)


def ragged_sizes(stream_key, amount, total, reach, skew):
    if amount == 2:
        one = jax.random.randint(stream_key, (), max(1, total - reach), min(reach, total - 1) + 1)
        return jnp.stack([one, total - one])
    tallies = jnp.asarray(length_profile(amount, total, reach, skew), jnp.int32)
    couples = (amount - 1) // 2
    giver, receiver = tallies[1:1 + 2 * couples:2], tallies[2:2 + 2 * couples:2]
    margin = jnp.minimum(giver - 1, reach - receiver)
    moved = jax.random.randint(jax.random.fold_in(stream_key, 1), (couples,), 0, 1 << 20) % (margin + 1)
    tallies = tallies.at[1:1 + 2 * couples:2].set(giver - moved).at[2:2 + 2 * couples:2].set(receiver + moved)
    return tallies[jax.random.permutation(jax.random.fold_in(stream_key, 2), amount)]


def bell_draw(own_key, shape, deviation, most, pieces=(), dtype=jnp.bfloat16):
    level = block_levels(own_key, shape, pieces, -0.22, 0.18) if pieces else 1.0
    entries = jax.random.normal(own_key, shape, jnp.float32) * deviation * level
    return jnp.minimum(jnp.maximum(entries, -most), most).astype(dtype)


def setup_inputs(seed: int = 0) -> dict:
    streams_of = jax.random.split(jax.random.key(seed), 16)
    inputs = bell_draw(streams_of[0], (MICRO, TOKENS, D), 1.0, 6.0, ((1, 8),))
    segments = jax.vmap(lambda own: jnp.searchsorted(jnp.cumsum(ragged_sizes(own, 4 * TOKENS // PACK, TOKENS, PACK, 1)), jnp.arange(TOKENS), side="right"))(jax.random.split(streams_of[1], MICRO)).reshape((MICRO, TOKENS)).astype(jnp.int32)
    cotangent = bell_draw(streams_of[2], (MICRO, TOKENS, D), 1.0, 6.0, ((1, 8),))
    query_weight = bell_draw(streams_of[3], (2, D, D), D ** -0.5, 0.21875, ((0, 2), (2, 2)))
    key_weight = bell_draw(streams_of[4], (2, D, D), D ** -0.5, 0.21875, ((0, 2), (2, 2)))
    value_weight = bell_draw(streams_of[5], (2, D, D), D ** -0.5, 0.21875, ((0, 2), (2, 2)))
    out_weight = bell_draw(streams_of[6], (2, D, D), (D // 8) ** -0.5, 0.625, ((0, 2), (1, 2)))
    hidden_weight = bell_draw(streams_of[7], (2, D, FF), D ** -0.5, 0.21875, ((0, 2), (2, 2)))
    down_weight = bell_draw(streams_of[8], (2, FF, D), FF ** -0.5, 0.109375, ((0, 2), (1, 2)))
    first_gain = jnp.clip(1.0 + 0.1 * jax.random.normal(streams_of[9], (2, D), jnp.float32), 0.5, 1.5)
    second_gain = jnp.clip(1.0 + 0.1 * jax.random.normal(streams_of[10], (2, D), jnp.float32), 0.5, 1.5)
    query_down = bell_draw(streams_of[11], (2, D, RANK), D ** -0.5, 0.21875, ((0, 2),))
    query_up = bell_draw(streams_of[12], (2, RANK, D), RANK ** -0.5, 2.0, ((0, 2), (2, 2)))
    value_down = bell_draw(streams_of[13], (2, D, RANK), D ** -0.5, 0.21875, ((0, 2),))
    value_up = bell_draw(streams_of[14], (2, RANK, D), RANK ** -0.5, 2.0, ((0, 2), (2, 2)))
    return {"inputs": inputs, "segments": segments, "cotangent": cotangent, "query_weight": query_weight, "key_weight": key_weight, "value_weight": value_weight, "out_weight": out_weight, "hidden_weight": hidden_weight, "down_weight": down_weight, "first_gain": first_gain, "second_gain": second_gain, "query_down": query_down, "query_up": query_up, "value_down": value_down, "value_up": value_up}


@jax.custom_vjp
def low(v):
    return lax.optimization_barrier(v.astype(jnp.bfloat16)).astype(jnp.float32)

@jax.custom_vjp
def low_back(v):
    return v

def low_keep(v):
    return (low(v), None)

def low_pass(kept, grad):
    return (grad,)

def back_keep(v):
    return (v, None)

def back_low(kept, grad):
    return (low(grad),)
low.defvjp(low_keep, low_pass)
low_back.defvjp(back_keep, back_low)
HIGHEST = lax.Precision.HIGHEST
EPS = 1e-05
MASKED = -1000000000.0

def matmul(matrix, factor):
    return jnp.dot(matrix, factor, precision=HIGHEST, preferred_element_type=jnp.float32)

def normalize(summed, norm_gain):
    center = summed - lax.optimization_barrier(jnp.mean(summed, axis=-1, keepdims=True))
    scale_row = lax.rsqrt(lax.optimization_barrier(jnp.mean(center * center, axis=-1, keepdims=True)) + EPS)
    return center * scale_row * norm_gain

def attention(queries, keys_all, values_all, allowed):
    length = queries.shape[0]
    head_count = queries.shape[1] // HEAD_DIM
    query_heads = queries.reshape(length, head_count, HEAD_DIM)
    key_heads = keys_all.reshape(length, head_count, HEAD_DIM)
    value_heads = values_all.reshape(length, head_count, HEAD_DIM)
    scores = low_back(jnp.einsum('qhd,khd->hqk', query_heads, key_heads, precision=HIGHEST) * HEAD_DIM ** (-0.5))
    masked = jnp.where(allowed[None], scores, MASKED)
    softened = low(jax.nn.softmax(masked, axis=-1))
    context = jnp.einsum('hqk,khd->qhd', softened, value_heads, precision=HIGHEST)
    return context.reshape(length, head_count * HEAD_DIM)

def encoder_layer(layer_in, allowed, params, adapters):
    query_weight, key_weight, value_weight, out_weight, hidden_weight, down_weight, first_gain, second_gain = params
    query_down, query_up, value_down, value_up = adapters
    query_low = low_back(low(matmul(layer_in, query_down)))
    value_low = low_back(low(matmul(layer_in, value_down)))
    queries = low_back(low(matmul(layer_in, query_weight) + matmul(query_low, query_up)))
    keys_all = low_back(low(matmul(layer_in, key_weight)))
    values_all = low_back(low(matmul(layer_in, value_weight) + matmul(value_low, value_up)))
    context = low_back(low(attention(queries, keys_all, values_all, allowed)))
    attended = low_back(matmul(context, out_weight))
    hidden = normalize(layer_in + attended, first_gain)
    hidden_low = low(hidden)
    before = low_back(matmul(hidden_low, hidden_weight))
    active = low(jax.nn.gelu(before))
    mixed_out = low_back(matmul(active, down_weight))
    return low(normalize(hidden + mixed_out, second_gain))

def to_wide(stacked):
    return stacked.astype(jnp.float32)

def reference(inputs, segments, cotangent, query_weight, key_weight, value_weight, out_weight, hidden_weight, down_weight, first_gain, second_gain, query_down, query_up, value_down, value_up):
    frozen = tuple((to_wide(stacked) for stacked in (query_weight, key_weight, value_weight, out_weight, hidden_weight, down_weight, first_gain, second_gain)))
    adapters = tuple((to_wide(stacked) for stacked in (query_down, query_up, value_down, value_up)))
    pack_count = MICRO * TOKENS // PACK
    groups = pack_count // 8
    input_blocks = to_wide(inputs).reshape(groups, 8, PACK, D)
    segment_blocks = segments.reshape(groups, 8, PACK)
    zero_blocks = jnp.zeros_like(input_blocks)

    def two_sections(adapter_all, block_in, block_zero, block_seg):
        allowed = block_seg[:, None] == block_seg[None, :]
        first_out = encoder_layer(block_in, allowed, tuple((stacked[0] for stacked in frozen)), tuple((stacked[0] for stacked in adapter_all)))
        second_in = low_back(first_out) + block_zero
        second_out = encoder_layer(second_in, allowed, tuple((stacked[1] for stacked in frozen)), tuple((stacked[1] for stacked in adapter_all)))
        return (first_out, second_out)

    def group_pass(adapter_all, block_in, block_zero, block_seg):
        return jax.vmap(two_sections, in_axes=(None, 0, 0, 0))(adapter_all, block_in, block_zero, block_seg)
    checked = jax.checkpoint(group_pass)

    def whole_pass(adapter_all, all_in, all_zero):
        return lax.map(lambda block_items: checked(adapter_all, block_items[0], block_items[1], block_items[2]), (all_in, all_zero, segment_blocks))
    outputs, pullback = jax.vjp(whole_pass, adapters, input_blocks, zero_blocks)
    cotangent_blocks = to_wide(cotangent).reshape(groups, 8, PACK, D)
    adapter_grads, grad_first, grad_second = pullback((jnp.zeros_like(outputs[0]), cotangent_blocks))
    full_shape = (MICRO, TOKENS, D)
    activations = jnp.stack([outputs[0].reshape(full_shape), outputs[1].reshape(full_shape)]).astype(jnp.bfloat16)
    input_grads = jnp.stack([grad_first.reshape(full_shape), grad_second.reshape(full_shape)]).astype(jnp.bfloat16)
    return (activations, input_grads, adapter_grads[0], adapter_grads[1], adapter_grads[2], adapter_grads[3])
```

```python
import jax
import jax.numpy as jnp
from jax import lax
from jax.sharding import PartitionSpec as P

HEAD_DIM = 64
EPS = 1e-05
MASKED = -1000000000.0


def swap(block, axis):
    return lax.ppermute(block, axis, [(0, 1), (1, 0)])


def core_swap(block):
    return lax.ppermute(block, "dp", [(i, i ^ 1) for i in range(lax.axis_size("dp"))])


def matmul(matrix, factor):
    return jnp.dot(matrix, factor, preferred_element_type=jnp.float32)


def contract(matrix, factor, matrix_dim, factor_dim):
    return lax.dot_general(
        matrix, factor, (((matrix_dim,), (factor_dim,)), ((), ())), preferred_element_type=jnp.float32
    )


def normalize(summed):
    center = summed - jnp.mean(summed, axis=-1, keepdims=True)
    scale_row = lax.rsqrt(jnp.mean(center * center, axis=-1, keepdims=True) + EPS)
    return (center * scale_row, scale_row)


def norm_back(grad_out, norm_gain, normed, scale_row):
    scaled = grad_out * norm_gain
    return scale_row * (
        scaled
        - jnp.mean(scaled, axis=-1, keepdims=True)
        - normed * jnp.mean(scaled * normed, axis=-1, keepdims=True)
    )


def heads_of(matrix):
    return matrix.reshape(matrix.shape[0], matrix.shape[1] // HEAD_DIM, HEAD_DIM)


def forward(layer_in, allowed, weights):
    (wq, wk, wv, wo, wh, wd, g1, g2, qd, qu, vd, vu) = weights
    query_low = matmul(layer_in, qd).astype(jnp.bfloat16)
    value_low = matmul(layer_in, vd).astype(jnp.bfloat16)
    queries = (matmul(layer_in, wq) + matmul(query_low, qu)).astype(jnp.bfloat16)
    keys_all = matmul(layer_in, wk).astype(jnp.bfloat16)
    values_all = (matmul(layer_in, wv) + matmul(value_low, vu)).astype(jnp.bfloat16)
    head_scale = HEAD_DIM ** (-0.5)
    scores = (
        jnp.einsum("qhd,khd->hqk", heads_of(queries), heads_of(keys_all), preferred_element_type=jnp.float32)
        * head_scale
    )
    masked = jnp.where(allowed[None], scores, MASKED)
    shifted = jnp.exp(masked - jnp.max(masked, axis=-1, keepdims=True))
    softened = shifted / jnp.sum(shifted, axis=-1, keepdims=True)
    softened_low = softened.astype(jnp.bfloat16)
    context = jnp.einsum("hqk,khd->qhd", softened_low, heads_of(values_all), preferred_element_type=jnp.float32)
    context_low = context.reshape(queries.shape).astype(jnp.bfloat16)
    first_normed, first_scale = normalize(layer_in.astype(jnp.float32) + matmul(context_low, wo))
    hidden = first_normed * g1
    before = matmul(hidden.astype(jnp.bfloat16), wh)
    active = jax.nn.gelu(before).astype(jnp.bfloat16)
    second_normed, second_scale = normalize(hidden + matmul(active, wd))
    result_low = (second_normed * g2).astype(jnp.bfloat16)
    saved = (query_low, value_low, queries, keys_all, values_all, softened, softened_low,
             first_normed, first_scale, before, second_normed, second_scale)
    return result_low, saved


def backward(layer_in, weights, grad_out, saved):
    (wq, wk, wv, wo, wh, wd, g1, g2, qd, qu, vd, vu) = weights
    (query_low, value_low, queries, keys_all, values_all, softened, softened_low,
     first_normed, first_scale, before, second_normed, second_scale) = saved
    head_scale = HEAD_DIM ** (-0.5)
    second_back = norm_back(grad_out, g2, second_normed, second_scale)
    grad_active = contract(second_back.astype(jnp.bfloat16), wd, 1, 1)
    gelu_pull = jax.vjp(jax.nn.gelu, before)[1]
    grad_before = gelu_pull(grad_active)[0].astype(jnp.bfloat16)
    grad_hidden = contract(grad_before, wh, 1, 1)
    first_back = norm_back(grad_hidden + second_back, g1, first_normed, first_scale)
    grad_context = contract(first_back.astype(jnp.bfloat16), wo, 1, 1).astype(jnp.bfloat16)
    context_heads = heads_of(grad_context)
    grad_soft = jnp.einsum("qhd,khd->hqk", context_heads, heads_of(values_all), preferred_element_type=jnp.float32)
    grad_scores = (softened * (grad_soft - jnp.sum(softened * grad_soft, axis=-1, keepdims=True))).astype(jnp.bfloat16)

    def back(spec, a, b, scale=1.0):
        return (jnp.einsum(spec, a, b, preferred_element_type=jnp.float32) * scale).reshape(queries.shape).astype(jnp.bfloat16)

    grad_queries = back("hqk,khd->qhd", grad_scores, heads_of(keys_all), head_scale)
    grad_keys = back("hqk,qhd->khd", grad_scores, heads_of(queries), head_scale)
    grad_values = back("hqk,qhd->khd", softened_low, context_heads)
    fq = contract(grad_queries, qu, 1, 1).astype(jnp.bfloat16)
    fv = contract(grad_values, vu, 1, 1).astype(jnp.bfloat16)
    grad_input = (
        contract(grad_queries, wq, 1, 1) + contract(grad_keys, wk, 1, 1) + contract(grad_values, wv, 1, 1)
        + first_back + contract(fq, qd, 1, 1) + contract(fv, vd, 1, 1)
    )
    terms = (
        contract(layer_in, fq, 0, 0), contract(query_low, grad_queries, 0, 0),
        contract(layer_in, fv, 0, 0), contract(value_low, grad_values, 0, 0),
    )
    return grad_input.astype(jnp.bfloat16), terms


def half_rows(matrix, which):
    count = matrix.shape[0] // 2
    return lax.dynamic_slice_in_dim(matrix, which * count, count, 0)


def gather_quarter(hop, own_half, core):
    got = hop(own_half)
    mate = core_swap(got)
    return jnp.concatenate([jnp.where(core == 0, got, mate), jnp.where(core == 0, mate, got)], 0)


def body(inputs, segments, cotangent, *stacked):
    section = lax.axis_index("section")
    tensor = lax.axis_index("tensor")
    core = lax.axis_index("dp") % 2
    own = [array[0] for array in stacked]

    def x_hop(v):
        return swap(v, "section")

    def y_hop(v):
        return swap(v, "tensor")

    big = [0, 1, 2, 3, 4, 5]
    own_big = {k: half_rows(own[k], core) for k in big}
    a_half = {k: y_hop(own_big[k]) for k in big}
    b_half = {k: x_hop(own_big[k]) for k in big}
    c_half = {k: x_hop(a_half[k]) for k in big}

    def whole(part):
        mate = core_swap(part)
        return jnp.concatenate([jnp.where(core == 0, part, mate), jnp.where(core == 0, mate, part)], 0)

    quarter_a = {k: whole(v) for k, v in a_half.items()}
    quarter_b = {k: whole(v) for k, v in b_half.items()}
    quarter_c = {k: whole(v) for k, v in c_half.items()}
    for k in (9, 11):
        quarter_a[k] = y_hop(own[k])
        quarter_b[k] = x_hop(own[k])
        quarter_c[k] = x_hop(quarter_a[k])
    axis_of = {0: 1, 1: 1, 2: 1, 3: 0, 4: 1, 5: 0, 9: 1, 11: 1}

    def layer(first):
        result = []
        for k in range(12):
            if k in axis_of:
                mine = jnp.concatenate([own[k], quarter_a[k]], axis_of[k])
                other = jnp.concatenate([quarter_b[k], quarter_c[k]], axis_of[k])
            else:
                mine, other = own[k], x_hop(own[k])
            result.append(jnp.where(section == first, mine, other))
        return tuple(result)

    weights = (layer(0), layer(1))
    pack = 2 * section + tensor
    take = lambda v: lax.dynamic_index_in_dim(v, pack, 0, keepdims=False)
    labels = take(segments)
    allowed = labels[:, None] == labels[None, :]
    x0 = take(inputs)
    act0, saved0 = forward(x0, allowed, weights[0])
    act1, saved1 = forward(act0, allowed, weights[1])
    ig1, terms1 = backward(act0, weights[1], take(cotangent).astype(jnp.float32), saved1)
    ig0, terms0 = backward(x0, weights[0], ig1.astype(jnp.float32), saved0)

    def spread(first, second):
        mine = jnp.where(section == 0, first, second)
        other = jnp.where(section == 0, second, first)
        parts = jnp.stack([
            half_rows(mine, tensor),
            y_hop(half_rows(mine, 1 - tensor)),
            x_hop(half_rows(other, tensor)),
            y_hop(x_hop(half_rows(other, 1 - tensor))),
        ])
        return jnp.stack([lax.dynamic_index_in_dim(parts, j ^ pack, 0, keepdims=False) for j in range(4)])[None]

    mine = [jnp.where(section == 0, a, b) for a, b in zip(terms0, terms1)]
    other = [jnp.where(section == 0, b, a) for a, b in zip(terms0, terms1)]
    total = [m + x_hop(o) for m, o in zip(mine, other)]
    ups = [jnp.add(*[f(h) for f, h in zip((lambda v: v, y_hop), jnp.split(total[k], 2, 1))]) for k in (1, 3)]
    downs = lax.psum((total[0], total[2]), ("dp", "tensor"))
    ups = lax.psum(ups, "dp")
    return (spread(act0, act1), spread(ig0, ig1), downs[0][None], ups[0][None], downs[1][None], ups[1][None])


def solution(mesh):
    return jax.shard_map(
        body,
        mesh=mesh,
        in_specs=(
            P(None, "dp", None), P(None, "dp"), P(None, "dp", None),
            P("section", None, "tensor"), P("section", None, "tensor"), P("section", None, "tensor"),
            P("section", "tensor", None), P("section", None, "tensor"), P("section", "tensor", None),
            P("section", None), P("section", None),
            P("section", None, None), P("section", None, "tensor"),
            P("section", None, None), P("section", None, "tensor"),
        ),
        out_specs=(
            P("section", None, ("dp", "tensor"), None), P("section", None, ("dp", "tensor"), None),
            P("section", None, None), P("section", None, "tensor"),
            P("section", None, None), P("section", None, "tensor"),
        ),
        check_vma=False,
    )
```

```python
import functools

import jax
import jax.numpy as jnp
from jax import lax
from jax.experimental import pallas as pl
from jax.experimental.pallas import tpu as pltpu
from jax.sharding import PartitionSpec as P

HEAD_DIM = 64
EPS = 1e-05
MASKED = -1000000000.0
LOW = jnp.bfloat16
WIDE = jnp.float32
PAIR = 2 * HEAD_DIM
HEAD_SCALE = HEAD_DIM ** (-0.5)
TANH_ONE = 0.7978845608028654
TANH_TWO = 0.044715 * TANH_ONE


def dot_nn(a, b):
    return lax.dot_general(a, b, (((1,), (0,)), ((), ())), preferred_element_type=WIDE)


def dot_nt(a, b):
    return lax.dot_general(a, b, (((1,), (1,)), ((), ())), preferred_element_type=WIDE)


def dot_tn(a, b):
    return lax.dot_general(a, b, (((0,), (0,)), ((), ())), preferred_element_type=WIDE)


def normalize(summed):
    center = summed - jnp.mean(summed, axis=-1, keepdims=True)
    scale_row = lax.rsqrt(jnp.mean(center * center, axis=-1, keepdims=True) + EPS)
    return center * scale_row, scale_row


def norm_back(grad_out, gain, normed, scale_row):
    scaled = grad_out * gain
    return scale_row * (
        scaled
        - jnp.mean(scaled, axis=-1, keepdims=True)
        - normed * jnp.mean(scaled * normed, axis=-1, keepdims=True)
    )


def low_lanes(rows, width, first):
    return lax.broadcasted_iota(jnp.int32, (rows, width), 1) < first


def projections(x, w_qkv, ad_down, ad_up, q, k, v, lows):
    rows = x.shape[0]
    rank2 = ad_down.shape[0]
    both = dot_nt(x[...], ad_down[...]).astype(LOW)
    lows[...] = both
    first = low_lanes(rows, rank2, rank2 // 2)
    q_low = jnp.where(first, both, jnp.zeros_like(both))
    v_low = jnp.where(first, jnp.zeros_like(both), both)
    width = w_qkv.shape[2]
    for c in range(0, width, 256):
        cut = slice(c, c + 256)
        full = dot_nn(x[...], w_qkv[0, :, cut]) + dot_nn(q_low, ad_up[:, cut])
        q[:, cut] = (full.astype(LOW).astype(WIDE) * HEAD_SCALE).astype(LOW)
        k[:, cut] = dot_nn(x[...], w_qkv[1, :, cut]).astype(LOW)
        v[:, cut] = (dot_nn(x[...], w_qkv[2, :, cut]) + dot_nn(v_low, ad_up[:, cut])).astype(LOW)


def pair_lanes(i):
    return pl.ds(pl.multiple_of(i * PAIR, PAIR), PAIR)


def loop_pairs(pairs, step):
    each = 3 if pairs % 3 == 0 else 1

    def some(j, carry):
        for u in range(each):
            step(j * each + u)
        return carry

    lax.fori_loop(0, pairs // each, some, 0)


def attention(q, k, v, bias, e, ctx, rinv):
    rows, width = q.shape
    first = low_lanes(rows, PAIR, HEAD_DIM)

    def step(i):
        at = pair_lanes(i)
        q2, k2 = q[:, at], k[:, at]
        v2 = jnp.concatenate([v[:, at], jnp.ones((rows, PAIR), LOW)], 1)
        outs = []
        for h in range(2):
            mine = first if h == 0 else ~first
            scores = dot_nt(jnp.where(mine, q2, jnp.zeros_like(q2)), k2) + bias[...]
            top = jnp.max(scores, axis=1, keepdims=True)
            weights = jnp.exp(scores - top).astype(LOW)
            e[2 * i + h] = weights
            outs.append(dot_nn(weights, v2))
        inverse = 1.0 / jnp.where(first, outs[0][:, PAIR:], outs[1][:, PAIR:])
        rinv[:, at] = inverse
        ctx[:, at] = (jnp.where(first, outs[0][:, :PAIR], outs[1][:, :PAIR]) * inverse).astype(LOW)

    loop_pairs(width // PAIR, step)


def attention_back(q, k, v, e, ctx, rinv, dctx, dq, dk, dv):
    rows, width = q.shape
    first = low_lanes(rows, PAIR, HEAD_DIM)

    def step(i):
        at = pair_lanes(i)
        q2, k2, v2 = q[:, at], k[:, at], v[:, at]
        scaled = dctx[:, at].astype(WIDE) * rinv[:, at]
        scaled_low = scaled.astype(LOW)
        product = scaled * ctx[:, at].astype(WIDE)
        parts_q, parts_k, parts_v = [], [], []
        for h in range(2):
            mine = first if h == 0 else ~first
            row_sum = jnp.sum(jnp.where(mine, product, 0.0), axis=1, keepdims=True)
            grad = dot_nt(jnp.where(mine, scaled_low, jnp.zeros_like(scaled_low)), v2)
            grad_scores = e[2 * i + h] * (grad - row_sum).astype(LOW)
            parts_q.append(dot_nn(grad_scores, k2))
            parts_k.append(dot_tn(grad_scores, q2))
            parts_v.append(dot_tn(e[2 * i + h], scaled_low))
        dq[:, at] = (jnp.where(first, parts_q[0], parts_q[1]) * HEAD_SCALE).astype(LOW)
        dk[:, at] = jnp.where(first, parts_k[0], parts_k[1]).astype(LOW)
        dv[:, at] = jnp.where(first, parts_v[0], parts_v[1]).astype(LOW)

    loop_pairs(width // PAIR, step)


def feed_in(hidden_low, w_hidden, active, slope):
    for c in range(0, w_hidden.shape[1], 512):
        cut = slice(c, c + 512)
        u = dot_nn(hidden_low, w_hidden[:, cut])
        square = u * u
        t = jnp.tanh(u * (TANH_ONE + TANH_TWO * square))
        share = 0.5 + 0.5 * t
        out = u * share
        active[:, cut] = out.astype(LOW)
        slope[:, cut] = (share + out * (1.0 - t) * (TANH_ONE + 3.0 * TANH_TWO * square)).astype(LOW)


def feed_back(grad_low, w_down, slope, grad_before):
    for c in range(0, w_down.shape[0], 512):
        cut = slice(c, c + 512)
        grad = dot_nt(grad_low, w_down[cut, :])
        grad_before[:, cut] = (grad * slope[:, cut].astype(WIDE)).astype(LOW)


def mask_bias(seg_row, seg_col, bias):
    bias[...] = jnp.where(seg_col[...] == seg_row[...], 0.0, MASKED)


OWN_NAMES = ("q", "k", "v", "o", "h", "d")
PART_NAMES = ("qkv", "o", "h", "d")


class Layer:
    def __init__(self, which, where, own, parts):
        self.which, self.where, self.own, self.parts = which, where, own, parts

    def places(self, name, half, part, dst):
        if name == "qkv":
            rows, cols = dst.shape[1] // 4, dst.shape[2] // 2
            return dst.at[:, pl.ds(pl.multiple_of(part * rows, 32), rows), half * cols:(half + 1) * cols]
        if name == "h":
            rows, cols = dst.shape[0] // 4, dst.shape[1] // 2
            return dst.at[pl.ds(pl.multiple_of(part * rows, 32), rows), half * cols:(half + 1) * cols]
        rows = dst.shape[0] // 8
        return dst.at[pl.ds(pl.multiple_of((4 * half + part) * rows, 32), rows), :]

    def start(self, name, dst, sem):
        holder = self.where[0] == self.which
        mine = self.where[1]

        def own_half():
            if name == "qkv":
                cols = dst.shape[2] // 2
                for j, one in enumerate("qkv"):
                    pltpu.make_async_copy(self.own[one].at[0], dst.at[j, :, 0:cols], sem).start()
            elif name == "h":
                pltpu.make_async_copy(self.own["h"].at[0], dst.at[:, 0:dst.shape[1] // 2], sem).start()
            else:
                pltpu.make_async_copy(self.own[name].at[0], dst.at[0:dst.shape[0] // 2, :], sem).start()

        def part_half(letter, half):
            for r in range(4):
                source = self.parts[letter][name][r]
                pltpu.make_async_copy(source, self.places(name, half, mine ^ r, dst), sem).start()

        @pl.when(holder)
        def _():
            own_half()
            part_half("A", 1)

        @pl.when(jnp.logical_not(holder))
        def _():
            part_half("B", 0)
            part_half("C", 1)

    def wait(self, dst, sem):
        pltpu.make_async_copy(dst, dst, sem).wait()


def weight_inputs(own, parts, names):
    flat, spots = [], []
    for name in names:
        for one in ("qkv" if name == "qkv" else (name,)):
            spots.append(("own", one, 0))
            flat.append(own[one])
        for letter in "ABC":
            for r in range(4):
                spots.append((letter, name, r))
                flat.append(parts[letter][name][r])

    def rebuild(refs):
        own_refs, part_refs = {}, {letter: {name: [None] * 4 for name in names} for letter in "ABC"}
        for ref, (letter, name, r) in zip(refs, spots):
            if letter == "own":
                own_refs[name] = ref
            else:
                part_refs[letter][name][r] = ref
        return own_refs, part_refs

    return flat, rebuild


VMEM = pl.BlockSpec(memory_space=pltpu.VMEM)
SMEM = pl.BlockSpec(memory_space=pltpu.SMEM)
HBM = pl.BlockSpec(memory_space=pl.ANY)


def call(kernel, small, flat, outs, scratch, flops, name):
    moved = sum(a.size * a.dtype.itemsize for a in list(small) + list(flat) + list(outs))
    return pl.pallas_call(
        kernel,
        out_shape=tuple(outs),
        in_specs=[SMEM] + [VMEM] * (len(small) - 1) + [HBM] * len(flat),
        out_specs=tuple([VMEM] * len(outs)),
        scratch_shapes=scratch,
        compiler_params=pltpu.CompilerParams(vmem_limit_bytes=60 * 2**20),
        cost_estimate=pl.CostEstimate(flops=flops, bytes_accessed=moved, transcendentals=0),
        name=name,
    )(*small, *flat)


def shape(dims, dtype):
    return jax.ShapeDtypeStruct(tuple(dims), dtype)


class Sizes:
    def __init__(self, rows, width, hidden, rank2):
        self.rows, self.width, self.hidden, self.rank2 = rows, width, hidden, rank2
        self.heads = width // HEAD_DIM

    def vmem(self, name):
        kept = dict(
            qkv=((3, self.width, self.width), LOW), o=((self.width, self.width), LOW),
            h=((self.width, self.hidden), LOW), d=((self.hidden, self.width), LOW),
            rows_low=((self.rows, self.width), LOW), rows=((self.rows, self.width), WIDE),
            e=((self.heads, self.rows, self.rows), LOW), bias=((self.rows, self.rows), WIDE),
            column=((self.rows, 1), WIDE), mid=((self.rows, self.hidden), LOW), lows=((self.rows, self.rank2), LOW),
        )
        return kept[name]

    def scratch(self, *names):
        return [pltpu.VMEM(*self.vmem(n)) for n in names]

    def out(self, *names):
        return [shape(*self.vmem(n)) for n in names]


def attention_call(sizes, where, x, seg_row, seg_col, ad_down, ad_up, gain, own, parts, layer):
    flat, rebuild = weight_inputs(own, parts, ("qkv", "o"))

    def kernel(where, x, seg_row, seg_col, ad_down, ad_up, gain, *rest):
        own_refs, part_refs = rebuild(rest[:len(flat)])
        q, k, v, e, rinv, ctx, n1, s1, lows, w_qkv, w_o, bias, sems = rest[len(flat):]
        loader = Layer(layer, where, own_refs, part_refs)
        loader.start("qkv", w_qkv, sems.at[0])
        loader.start("o", w_o, sems.at[1])
        mask_bias(seg_row, seg_col, bias)
        loader.wait(w_qkv, sems.at[0])
        projections(x, w_qkv, ad_down, ad_up, q, k, v, lows)
        attention(q, k, v, bias, e, ctx, rinv)
        loader.wait(w_o, sems.at[1])
        normed, scale_row = normalize(x[...].astype(WIDE) + dot_nn(ctx[...], w_o[...]))
        n1[...] = normed
        s1[...] = scale_row

    outs = sizes.out("rows_low", "rows_low", "rows_low", "e", "rows", "rows_low", "rows", "column", "lows")
    flops = 2 * sizes.rows * sizes.width * (4 * sizes.width + 4 * sizes.rows)
    return call(kernel, (where, x, seg_row, seg_col, ad_down, ad_up, gain), flat, outs,
                sizes.scratch("qkv", "o", "bias") + [pltpu.SemaphoreType.DMA((2,))], flops, "attention_first")


def feed_in_call(sizes, where, n1, gain, own, parts, layer):
    flat, rebuild = weight_inputs(own, parts, ("h",))

    def kernel(where, n1, gain, *rest):
        own_refs, part_refs = rebuild(rest[:len(flat)])
        active, slope, w_h, sems = rest[len(flat):]
        loader = Layer(layer, where, own_refs, part_refs)
        loader.start("h", w_h, sems.at[0])
        loader.wait(w_h, sems.at[0])
        feed_in((n1[...] * gain[...]).astype(LOW), w_h, active, slope)

    flops = 2 * sizes.rows * sizes.width * sizes.hidden
    return call(kernel, (where, n1, gain), flat, sizes.out("mid", "mid"),
                sizes.scratch("h") + [pltpu.SemaphoreType.DMA((1,))], flops, "feed_in_first")


def feed_out_call(sizes, where, active, n1, gain, gain2, own, parts, layer):
    flat, rebuild = weight_inputs(own, parts, ("d",))

    def kernel(where, active, n1, gain, gain2, *rest):
        own_refs, part_refs = rebuild(rest[:len(flat)])
        act, n2, s2, w_d, sems = rest[len(flat):]
        loader = Layer(layer, where, own_refs, part_refs)
        loader.start("d", w_d, sems.at[0])
        loader.wait(w_d, sems.at[0])
        normed, scale_row = normalize(n1[...] * gain[...] + dot_nn(active[...], w_d[...]))
        n2[...] = normed
        s2[...] = scale_row
        act[...] = (normed * gain2[...]).astype(LOW)

    flops = 2 * sizes.rows * sizes.width * sizes.hidden
    return call(kernel, (where, active, n1, gain, gain2), flat, sizes.out("rows_low", "rows", "column"),
                sizes.scratch("d") + [pltpu.SemaphoreType.DMA((1,))], flops, "feed_out_first")


def back_pieces(x, grad_out, gain, gain2, ad_down, ad_up, w, saved, work, grad_in, terms, ready):
    q, k, v, e, rinv, ctx, n1, s1, n2, s2, slope, lows = saved
    mid, dctx, dq, dk, dv = work
    second_back = norm_back(grad_out, gain2[...], n2[...], s2[...])
    ready("d")
    feed_back(second_back.astype(LOW), w["d"], slope, mid)
    ready("h")
    grad_hidden = dot_nt(mid[...], w["h"][...])
    first_back = norm_back(grad_hidden + second_back, gain[...], n1[...], s1[...])
    ready("o")
    dctx[...] = dot_nt(first_back.astype(LOW), w["o"][...]).astype(LOW)
    ready("saved")
    attention_back(q, k, v, e, ctx, rinv, dctx, dq, dk, dv)
    ready("qkv")
    rows, rank2 = lows.shape
    first = low_lanes(rows, rank2, rank2 // 2)
    factor = jnp.where(first, dot_nt(dq[...], ad_up[...]), dot_nt(dv[...], ad_up[...])).astype(LOW)
    grad_in[...] = (
        dot_nt(dq[...], w["qkv"][0]) + dot_nt(dk[...], w["qkv"][1]) + dot_nt(dv[...], w["qkv"][2])
        + first_back + dot_nn(factor, ad_down[...])
    ).astype(LOW)
    terms[0:rank2, :] = dot_tn(factor, x[...])
    up = lax.broadcasted_iota(jnp.int32, (rank2, x.shape[1]), 0) < rank2 // 2
    terms[rank2:2 * rank2, :] = jnp.where(up, dot_tn(lows[...], dq[...]), dot_tn(lows[...], dv[...]))


def second_call(sizes, where, x, seg_row, seg_col, cot, ad_down, ad_up, gain, gain2, own, parts, layer):
    flat, rebuild = weight_inputs(own, parts, PART_NAMES)

    def kernel(where, x, seg_row, seg_col, cot, ad_down, ad_up, gain, gain2, *rest):
        own_refs, part_refs = rebuild(rest[:len(flat)])
        (act, grad_in, terms, w_qkv, w_o, w_h, w_d, bias, q, k, v, e, rinv, ctx, n1, s1, n2, s2, slope, mid, lows,
         dctx, dq, dk, dv, sems) = rest[len(flat):]
        loader = Layer(layer, where, own_refs, part_refs)
        w = dict(qkv=w_qkv, o=w_o, h=w_h, d=w_d)
        for j, name in enumerate(PART_NAMES):
            loader.start(name, w[name], sems.at[j])
        mask_bias(seg_row, seg_col, bias)
        loader.wait(w_qkv, sems.at[0])
        projections(x, w_qkv, ad_down, ad_up, q, k, v, lows)
        attention(q, k, v, bias, e, ctx, rinv)
        loader.wait(w_o, sems.at[1])
        normed, scale_row = normalize(x[...].astype(WIDE) + dot_nn(ctx[...], w_o[...]))
        n1[...] = normed
        s1[...] = scale_row
        hidden = normed * gain[...]
        loader.wait(w_h, sems.at[2])
        feed_in(hidden.astype(LOW), w_h, mid, slope)
        loader.wait(w_d, sems.at[3])
        normed, scale_row = normalize(n1[...] * gain[...] + dot_nn(mid[...], w_d[...]))
        n2[...] = normed
        s2[...] = scale_row
        act[...] = (normed * gain2[...]).astype(LOW)
        back_pieces(x, cot[...].astype(WIDE), gain, gain2, ad_down, ad_up, w,
                    (q, k, v, e, rinv, ctx, n1, s1, n2, s2, slope, lows), (mid, dctx, dq, dk, dv),
                    grad_in, terms, lambda name: None)

    outs = sizes.out("rows_low", "rows_low") + [shape((2 * sizes.rank2, sizes.width), WIDE)]
    scratch = sizes.scratch(
        "qkv", "o", "h", "d", "bias", "rows_low", "rows_low", "rows_low", "e", "rows", "rows_low", "rows", "column",
        "rows", "column", "mid", "mid", "lows", "rows_low", "rows_low", "rows_low", "rows_low")
    flops = 4 * sizes.rows * sizes.width * (4 * sizes.width + 2 * sizes.hidden + 6 * sizes.rows)
    return call(kernel, (where, x, seg_row, seg_col, cot, ad_down, ad_up, gain, gain2), flat, outs,
                scratch + [pltpu.SemaphoreType.DMA((4,))], flops, "second_layer")


def first_back_call(sizes, where, x, grad_out, n2, s2, ad_down, ad_up, gain, gain2, saved, own, parts, layer):
    flat, rebuild = weight_inputs(own, parts, PART_NAMES)
    kept = list(saved)
    names = ("rows_low", "rows_low", "rows_low", "e", "rows", "rows_low", "rows", "column", "mid", "lows")

    def kernel(where, x, grad_out, n2, s2, ad_down, ad_up, gain, gain2, *rest):
        sources = rest[:len(kept)]
        rest = rest[len(kept):]
        own_refs, part_refs = rebuild(rest[:len(flat)])
        (grad_in, terms, w_qkv, w_o, w_h, w_d, q, k, v, e, rinv, ctx, n1, s1, slope, lows,
         mid, dctx, dq, dk, dv, sems) = rest[len(flat):]
        loader = Layer(layer, where, own_refs, part_refs)
        w = dict(qkv=w_qkv, o=w_o, h=w_h, d=w_d)
        homes = (q, k, v, e, rinv, ctx, n1, s1, slope, lows)
        copies = [pltpu.make_async_copy(s, d, sems.at[4 + j]) for j, (s, d) in enumerate(zip(sources, homes))]
        loader.start("d", w_d, sems.at[3])
        copies[8].start()
        loader.start("h", w_h, sems.at[2])
        copies[6].start()
        copies[7].start()
        loader.start("o", w_o, sems.at[1])
        for j in (2, 3, 4, 5, 1, 0, 9):
            copies[j].start()
        loader.start("qkv", w_qkv, sems.at[0])

        def ready(name):
            if name == "d":
                loader.wait(w_d, sems.at[3])
                copies[8].wait()
            elif name == "h":
                loader.wait(w_h, sems.at[2])
                copies[6].wait()
                copies[7].wait()
            elif name == "o":
                loader.wait(w_o, sems.at[1])
            elif name == "saved":
                for j in (2, 3, 4, 5, 1, 0, 9):
                    copies[j].wait()
            else:
                loader.wait(w_qkv, sems.at[0])

        back_pieces(x, grad_out[...].astype(WIDE), gain, gain2, ad_down, ad_up, w,
                    (q, k, v, e, rinv, ctx, n1, s1, n2, s2, slope, lows), (mid, dctx, dq, dk, dv),
                    grad_in, terms, ready)

    outs = sizes.out("rows_low") + [shape((2 * sizes.rank2, sizes.width), WIDE)]
    scratch = sizes.scratch("qkv", "o", "h", "d") + sizes.scratch(*names) + sizes.scratch(
        "mid", "rows_low", "rows_low", "rows_low", "rows_low")
    flops = 2 * sizes.rows * sizes.width * (4 * sizes.width + 2 * sizes.hidden + 8 * sizes.rows)
    return call(kernel, (where, x, grad_out, n2, s2, ad_down, ad_up, gain, gain2), kept + flat, outs,
                scratch + [pltpu.SemaphoreType.DMA((4 + len(kept),))], flops, "first_layer_back")


def flip(block, axes, bits):
    sizes = [lax.axis_size(a) for a in axes]
    route = []

    def flat(index):
        total = 0
        for i, n in zip(index, sizes):
            total = total * n + i
        return total

    places = [()]
    for n in sizes:
        places = [p + (i,) for p in places for i in range(n)]
    for p in places:
        route.append((flat(p), flat(tuple(i ^ b for i, b in zip(p, bits)))))
    return lax.ppermute(block, axes, route)


def x_hop(v):
    return flip(v, ("section",), (1,))


def y_hop(v):
    return flip(v, ("tensor",), (1,))


def diagonal_hop(v):
    return flip(v, ("section", "tensor"), (1, 1))


def dp_hop(v, bits):
    return flip(v, ("dp",), (bits,))


def cut_rows(matrix, count, index, axis=0):
    rows = matrix.shape[axis] // count
    return lax.dynamic_slice_in_dim(matrix, index * rows, rows, axis)


def gather_parts(own, mine):
    parts = {letter: {} for letter in "ABC"}
    for name in PART_NAMES:
        if name == "qkv":
            piece = jnp.stack([cut_rows(own[one][0], 4, mine) for one in "qkv"])
        else:
            piece = cut_rows(own[name][0], 4, mine)
        a0 = y_hop(piece)
        b0 = x_hop(piece)
        a2 = dp_hop(a0, 2)
        b2 = dp_hop(b0, 2)
        c0 = y_hop(b0)
        c2 = x_hop(a2)
        for letter, zero, two in (("A", a0, a2), ("B", b0, b2), ("C", c0, c2)):
            parts[letter][name] = [zero, dp_hop(zero, 1), two, dp_hop(two, 1)]
    return parts


def sum_terms(terms):
    core = lax.axis_index("dp") % 2
    half = cut_rows(terms, 2, core) + dp_hop(cut_rows(terms, 2, 1 - core), 1)
    half = half + x_hop(half) + y_hop(half) + diagonal_hop(half)
    bits = lax.axis_size("dp").bit_length() - 1
    at = 1
    while at < bits:
        if at + 1 < bits:
            one, two = 1 << at, 2 << at
            half = half + dp_hop(half, one) + dp_hop(half, two) + dp_hop(half, one + two)
            at += 2
        else:
            half = half + dp_hop(half, 1 << at)
            at += 1
    mate = dp_hop(half, 1)
    return jnp.concatenate([jnp.where(core == 0, half, mate), jnp.where(core == 0, mate, half)], 0)


def body(inputs, segments, cotangent, wq, wk, wv, wo, wh, wd, first_gain, second_gain, qd, qu, vd, vu):
    section = lax.axis_index("section")
    tensor = lax.axis_index("tensor")
    mine = lax.axis_index("dp") % 4
    where = jnp.stack([section, mine]).astype(jnp.int32)
    own = dict(q=wq, k=wk, v=wv, o=wo, h=wh, d=wd)
    rank = qd.shape[2]
    sizes = Sizes(inputs.shape[1], inputs.shape[2], 2 * wh.shape[2], 2 * rank)

    downs = jnp.concatenate([qd[0].T, vd[0].T], 0)
    ups = jnp.concatenate([qu[0], vu[0]], 0)
    ups_mate = y_hop(ups)
    small = jnp.concatenate([downs, ups, ups_mate], 1)
    gains = jnp.concatenate([first_gain, second_gain], 0)
    small_other = x_hop(small)
    gains_other = x_hop(gains)
    width = sizes.width

    def pick(layer, here, there):
        return jnp.where(section == layer, here, there)

    adapters = []
    for layer in range(2):
        both = pick(layer, small, small_other)
        gain = pick(layer, gains, gains_other)
        adapters.append((both[:, :width], both[:, width:], gain[0:1], gain[1:2]))

    parts = gather_parts(own, mine)

    pack = 2 * section + tensor
    take = lambda a: lax.dynamic_index_in_dim(a, pack, 0, keepdims=False)
    labels = take(segments)
    seg_row, seg_col = labels[None, :], labels[:, None]
    x0 = take(inputs)
    cot = take(cotangent)

    down0, up0, gain0, gain20 = adapters[0]
    down1, up1, gain1, gain21 = adapters[1]
    q, k, v, e, rinv, ctx, n1, s1, lows = attention_call(
        sizes, where, x0, seg_row, seg_col, down0, up0, gain0, own, parts, 0)
    active, slope = feed_in_call(sizes, where, n1, gain0, own, parts, 0)
    act0, n2, s2 = feed_out_call(sizes, where, active, n1, gain0, gain20, own, parts, 0)
    act1, ig1, terms1 = second_call(
        sizes, where, act0, seg_row, seg_col, cot, down1, up1, gain1, gain21, own, parts, 1)
    ig0, terms0 = first_back_call(
        sizes, where, x0, ig1, n2, s2, down0, up0, gain0, gain20,
        (q, k, v, e, rinv, ctx, n1, s1, slope, lows), own, parts, 0)

    def spread(first, second):
        here = jnp.where(section == 0, first, second)
        there = jnp.where(section == 0, second, first)
        blocks = jnp.stack([
            cut_rows(here, 2, tensor),
            y_hop(cut_rows(here, 2, 1 - tensor)),
            x_hop(cut_rows(there, 2, tensor)),
            diagonal_hop(cut_rows(there, 2, 1 - tensor)),
        ])
        return jnp.stack([lax.dynamic_index_in_dim(blocks, j ^ pack, 0, keepdims=False) for j in range(4)])[None]

    def in_order(terms):
        down, up = terms[:2 * rank], terms[2 * rank:]
        return jnp.concatenate([down, jnp.where(tensor == 0, up, jnp.roll(up, width // 2, 1))], 0)

    total = jnp.where(section == 1, sum_terms(in_order(terms1)), sum_terms(in_order(terms0)))
    ups_total = cut_rows(total[2 * rank:], 2, tensor, 1)
    return (
        spread(act0, act1), spread(ig0, ig1),
        total[:rank].T[None], ups_total[:rank][None],
        total[rank:2 * rank].T[None], ups_total[rank:][None],
    )


def solution(mesh):
    return jax.shard_map(
        body,
        mesh=mesh,
        in_specs=(
            P(None, "dp", None), P(None, "dp"), P(None, "dp", None),
            P("section", None, "tensor"), P("section", None, "tensor"), P("section", None, "tensor"),
            P("section", "tensor", None), P("section", None, "tensor"), P("section", "tensor", None),
            P("section", None), P("section", None),
            P("section", None, None), P("section", None, "tensor"),
            P("section", None, None), P("section", None, "tensor"),
        ),
        out_specs=(
            P("section", None, ("dp", "tensor"), None), P("section", None, ("dp", "tensor"), None),
            P("section", None, None), P("section", None, "tensor"),
            P("section", None, None), P("section", None, "tensor"),
        ),
        check_vma=False,
    )
```
